512 devices in a mesh: gx: 8 (over y_hi, core), gy: 8 (over z), gz: 8 (over x, y_lo).
Axes of the slice: x: 4, y: 8 (y_hi: 4, y_lo: 2; y = y_hi * 2 + y_lo), z: 8, core: 2. Of those that a mesh axis runs over, the one named last changes fastest.
Arguments:
- orbital_values: bfloat16 [128, 128, 192, 384], P('gx', 'gy', 'gz'), may hold values from -6 to 6
- dm_slabs: bfloat16 [24576, 8, 384], P(('gx', 'gy', 'gz')), may hold values from -0.015625 to 0.015625
- slab_tile: int32 [24576], P(('gx', 'gy', 'gz')), may hold values from 0 to 63, as said below
- slab_place: int32 [24576], P(('gx', 'gy', 'gz')), may hold values from 0 to 47, as said below
Outputs:
- potential: float32 [128, 128, 192], P('gx', 'gy', 'gz')
- pot_slabs: bfloat16 [24576, 8, 384], P(('gx', 'gy', 'gz'))
The draws below stay inside these ranges and needn't reach their ends.
Inputs may be any that keep to these rules, and one draw needn't show every extreme that they name: `slab_tile`: within each layer along gz, every tile of that layer has exactly one slab for each place 0 .. 47, held by devices of the same layer; no device holds more than 2 slabs of one tile, and in every layer some device holds exactly 2 slabs of some tile. See slab_tile: the pair (slab_tile, slab_place) is different for all slabs of one layer.
All inputs are finite; a program needn't handle non-finite values.
Results may differ from the reference program's by a relative error of at most 0.0023.
Values may be sent and summed in bfloat16 or wider, within the bound.
A program may use at most 64 MiB of HBM per device.

```python
import math
import jax
import jax.numpy as jnp
import numpy as np
from jax import lax

TX = 16
TY = 16
TZ = 24
RADIUS = 8
ATOM_ORB = 8
LIST_BLK = 48
LIST_ORB = 384
CAP = 2
NX = 128
NY = 128
NZ = 192
SLABS = 24576
N_GX = 8
N_GY = 8
N_GZ = 8


def route_tables(key):
    tile_count = N_GX * N_GY
    surplus = LIST_BLK - CAP
    spread = min(tile_count - 1, surplus)
    base_count = surplus // spread
    leftover = surplus - base_count * spread
    counts = [CAP] + [base_count + 1] * leftover + [base_count] * (spread - leftover)
    offset_index = jnp.asarray(np.repeat(np.arange(len(counts)), counts).astype(np.int32))

    def one_layer(layer_key):
        key_shift, key_label, key_order, key_list = jax.random.split(layer_key, 4)
        shifts = jax.random.permutation(key_shift, tile_count)[:len(counts)].astype(jnp.int32)
        relabel = jax.random.permutation(key_label, tile_count).astype(jnp.int32)
        scores = jax.random.randint(key_order, (tile_count, LIST_BLK), 0, 1 << 20) * LIST_BLK + jnp.arange(LIST_BLK, dtype=jnp.int32)[None, :]
        shuffled = jnp.argsort(scores, axis=1, stable=True).astype(jnp.int32)
        chosen = offset_index[shuffled]
        owners = relabel[(jnp.arange(tile_count, dtype=jnp.int32)[:, None] + shifts[chosen]) % tile_count]
        tiebreak = jax.random.permutation(key_list, tile_count * LIST_BLK).astype(jnp.int32)
        ordering = jnp.argsort(owners.reshape(-1) * (tile_count * LIST_BLK) + tiebreak, stable=True).astype(jnp.int32)
        return ((ordering // LIST_BLK).reshape(tile_count, LIST_BLK), (ordering % LIST_BLK).reshape(tile_count, LIST_BLK))
    tile_ids, place_ids = jax.vmap(one_layer)(jax.random.split(key, N_GZ))
    return (tile_ids.transpose(1, 0, 2).reshape(-1), place_ids.transpose(1, 0, 2).reshape(-1))


def draw_slab_tile(key, part):
    return route_tables(jax.random.fold_in(key, 11))[0]


def draw_slab_place(key, part):
    return route_tables(jax.random.fold_in(key, 11))[1]


def block_scale(key, extent, shards, least, largest):
    def one(axis_at, parts):
        heights = jax.random.uniform(jax.random.fold_in(jax.random.fold_in(key, 6), axis_at), (parts,), jnp.float32, least / len(shards), largest / len(shards))
        return jnp.repeat(jnp.exp(heights), extent[axis_at] // parts).reshape((-1,) + (1,) * (len(extent) - axis_at - 1))

    level = one(*shards[0])
    for cut in shards[1:]:
        level = level * one(*cut)
    return level


def centred(own_key, extent, scale, reach, shards=(), kind=jnp.bfloat16):
    entries = jax.random.normal(own_key, extent, jnp.float32) * scale
    if len(shards) > 0:
        entries = block_scale(own_key, extent, shards, -0.22, 0.18) * entries
    return jnp.clip(entries, min=-reach, max=reach).astype(kind)


def setup_inputs(seed: int = 0) -> dict:
    arg_keys = jax.random.split(jax.random.key(seed), 5)
    return {
        "orbital_values": centred(arg_keys[0], (NX, NY, NZ, LIST_ORB), 1.0, 6.0, ((0, 8), (1, 8), (2, 8))),
        "dm_slabs": centred(arg_keys[1], (SLABS, ATOM_ORB, LIST_ORB), (LIST_ORB * LIST_ORB) ** -0.5, 0.015625, ((0, 512),)),
        "slab_tile": draw_slab_tile(jax.random.fold_in(arg_keys[4], 71), 0),
        "slab_place": draw_slab_place(jax.random.fold_in(arg_keys[4], 71), 0),
    }


ALPHAS = (0.012, 0.025, 0.05, 0.1, 0.2, 0.4, 0.8, 1.6)
MIXES = (0.30, 0.30, 0.32, 0.34, 0.36, 0.38, 0.40, 0.42)


def kernel_tables(radius):
    tap_table = [[math.exp(-alpha * offset * offset) for offset in range(-radius, radius + 1)] for alpha in ALPHAS]
    mix = [MIXES[term] / (sum(tap * tap for tap in tap_table[term]) ** 1.5) for term in range(len(ALPHAS))]
    return tap_table, mix


def smooth_periodic(density, radius):
    tap_table, mix = kernel_tables(radius)
    potential = None
    for term_idx in range(len(ALPHAS)):
        current = density
        for axis_idx in range(3):
            running = None
            for offset in range(2 * radius + 1):
                addend = tap_table[term_idx][offset] * jnp.roll(current, radius - offset, axis=axis_idx)
                running = addend if running is None else running + addend
            current = running
        addend = mix[term_idx] * current
        potential = addend if potential is None else potential + addend
    return potential


def reference(orbital_values, dm_slabs, slab_tile, slab_place):
    devices = N_GX * N_GY * N_GZ
    tile_pts = TX * TY * TZ
    row_width = ATOM_ORB * LIST_ORB
    owner_dev = jnp.arange(devices * LIST_BLK, dtype=jnp.int32) // LIST_BLK
    layer_idx = owner_dev % N_GZ
    target_row = ((slab_tile * N_GZ + layer_idx) * LIST_BLK + slab_place).astype(jnp.int32)
    inverse = jnp.zeros((devices * LIST_BLK,), jnp.int32).at[target_row].set(jnp.arange(devices * LIST_BLK, dtype=jnp.int32))
    tile_matrices = dm_slabs.reshape(devices * LIST_BLK, row_width)[inverse].reshape(devices, LIST_ORB, LIST_ORB)
    tile_values = orbital_values.reshape(N_GX, TX, N_GY, TY, N_GZ, TZ, LIST_ORB).transpose(0, 2, 4, 1, 3, 5, 6).reshape(devices, tile_pts, LIST_ORB)

    def density_of(operands):
        values, matrix = operands
        product = jnp.dot(values, matrix, preferred_element_type=jnp.float32)
        return jnp.sum(product * values.astype(jnp.float32), axis=1)

    densities = lax.map(density_of, (tile_values, tile_matrices))
    grid_density = densities.reshape(N_GX, N_GY, N_GZ, TX, TY, TZ).transpose(0, 3, 1, 4, 2, 5).reshape(NX, NY, NZ)
    potential = smooth_periodic(grid_density, RADIUS)
    tile_field = potential.reshape(N_GX, TX, N_GY, TY, N_GZ, TZ).transpose(0, 2, 4, 1, 3, 5).reshape(devices, tile_pts)
    quad_weight = float(tile_pts) ** -0.5

    def potential_of(operands):
        values, field_vals = operands
        weighted = (field_vals[:, None] * values.astype(jnp.float32) * quad_weight).astype(jnp.bfloat16)
        return lax.dot_general(values, weighted, (((0,), (0,)), ((), ())), preferred_element_type=jnp.float32).astype(jnp.bfloat16)

    tile_potentials = lax.map(potential_of, (tile_values, tile_field))
    pot_slabs = tile_potentials.reshape(devices * LIST_BLK, ATOM_ORB, LIST_ORB)[target_row]
    return potential, pot_slabs
```

```python
import functools
import math

import jax
import jax.numpy as jnp
import numpy as np
from jax import lax
from jax.experimental import pallas as pl
from jax.experimental.pallas import tpu as pltpu
from jax.sharding import PartitionSpec as P

MESH = pl.DeviceIdType.MESH
RADIUS = 8
ALPHAS = (0.012, 0.025, 0.05, 0.1, 0.2, 0.4, 0.8, 1.6)
MIXES = (0.30, 0.30, 0.32, 0.34, 0.36, 0.38, 0.40, 0.42)
TERMS = len(ALPHAS)
F32 = jnp.float32
BF16 = jnp.bfloat16
I32 = jnp.int32


def filter_tables(tx):
    taps = np.array([[math.exp(-a * s * s) for s in range(RADIUS + 1)] for a in ALPHAS])
    norm = taps[:, 0] ** 2 + 2 * (taps[:, 1:] ** 2).sum(axis=1)
    mix = np.array(MIXES) / norm**1.5
    along_x = np.zeros((tx + 2 * RADIUS, TERMS, tx))
    for x in range(tx):
        for s in range(-RADIUS, RADIUS + 1):
            along_x[x + RADIUS + s, :, x] = taps[:, abs(s)]
    along_x = along_x.reshape(tx + 2 * RADIUS, TERMS * tx).astype(np.float32)
    lanes = np.zeros((32, TERMS * tx), np.float32)
    lanes[: RADIUS + 1] = np.repeat(taps, tx, axis=0).T
    lanes[16 : 16 + RADIUS + 1] = np.repeat(taps * mix[:, None], tx, axis=0).T
    return along_x, lanes


def iota(shape, dim):
    return lax.broadcasted_iota(I32, shape, dim)


def one_hot(mask):
    return jnp.where(mask, 1.0, 0.0).astype(BF16)


def split(a):
    high = a.astype(BF16)
    return high, (a - high.astype(F32)).astype(BF16)


def dot(a, b, ca=1, cb=0):
    return lax.dot_general(a, b, (((ca,), (cb,)), ((), ())), preferred_element_type=F32)


def kernel(
    dims,
    v_hbm, dm_hbm, tile_ref, place_ref, xmat_ref, taps_ref,
    pot_ref, own_ref,
    v, dm, vp, vtp, perm, hot_out, hot_out_t, hot_in, hot_in_t,
    key_out, key_in, out_buf, in_buf, ret_buf, back_buf,
    tmat, acc, halo, fx, fz, pot,
    local_sem, key_send, key_recv, pay_send, pay_recv,
    ret_send, ret_recv, halo_send, halo_recv,
):
    (nx, ny, nz), (tx, ty, tz), count, orb = dims
    tiles = nx * ny
    points = ty * tz
    gx, gy, gz = lax.axis_index("gx"), lax.axis_index("gy"), lax.axis_index("gz")
    me = gx * ny + gy

    def peer(step):
        px = lax.rem(gx + step // ny, nx)
        py = lax.rem(gy + lax.rem(step, ny), ny)
        return px, py, px * ny + py

    def near(d):
        return tuple(
            lax.rem(at + by + size, size) for at, by, size in zip((gx, gy, gz), d, (nx, ny, nz))
        )

    neighbours = [
        (dx, dy, dz)
        for dz in (0, 1, -1)
        for dy in (0, 1, -1)
        for dx in (0, 1, -1)
        if (dx, dy, dz) != (0, 0, 0)
    ]
    others = [d for d in neighbours if d[2] != 0]

    load_dm = pltpu.make_async_copy(dm_hbm, dm, local_sem.at[0])
    load_dm.start()
    load_v = pltpu.make_async_copy(v_hbm, v, local_sem.at[1])
    load_v.start()
    barrier = pltpu.get_barrier_semaphore()

    def greet(step, carry):
        px, py, _ = peer(step)
        pl.semaphore_signal(barrier, inc=1, device_id=(px, py, gz), device_id_type=MESH)
        return carry

    lax.fori_loop(1, tiles, greet, 0)
    for d in others:
        pl.semaphore_signal(barrier, inc=1, device_id=near(d), device_id_type=MESH)

    owners = tile_ref[...]
    places = place_ref[...].astype(F32) + 1.0
    mine = one_hot(iota((tiles, count), 0) == owners)
    before = one_hot(iota((count, count), 0) < iota((count, count), 1))
    rank = jnp.sum(dot(mine, before) * mine.astype(F32), axis=0, keepdims=True)
    slot = 2.0 * owners.astype(F32) + rank
    spread = one_hot(iota((count, orb), 1) // 8 == iota((count, orb), 0))
    wide = dot(jnp.broadcast_to(slot, (8, count)).astype(BF16), spread)[0:1]
    slot_row = (wide * 8.0).astype(I32) + (iota((1, orb), 1) & 7)
    for s in range(2):
        chosen = iota((tiles, count), 0) * 2 + s == slot.astype(I32)
        listed = jnp.where(chosen, places, 0.0).astype(BF16)
        key_out[:, s, :] = dot(listed, jnp.ones((count, 128), BF16))
    load_dm.wait()
    rows = 256

    def pack(i, carry):
        at = pl.ds(pl.multiple_of(i * rows, rows), rows)
        hot = one_hot(iota((rows, orb), 0) + i * rows == slot_row)
        hot_out[at, :] = hot
        out_buf[at, :] = dot(hot, dm[...]).astype(BF16)
        return carry

    lax.fori_loop(0, tiles * 16 // rows, pack, 0)

    pl.semaphore_wait(barrier, tiles - 1 + len(others))

    def block(ref, at):
        return ref.at[pl.ds(pl.multiple_of(at * 16, 16), 16), :]

    def send_keys(step, carry):
        px, py, at = peer(step)
        pltpu.make_async_remote_copy(
            src_ref=key_out.at[at], dst_ref=key_in.at[me], send_sem=key_send, recv_sem=key_recv,
            device_id=(px, py, gz), device_id_type=MESH,
        ).start()
        return carry

    def sender(src, dst, send_sem, recv_sem):
        def send(step, carry):
            px, py, at = peer(step)
            pltpu.make_async_remote_copy(
                src_ref=block(src, at), dst_ref=block(dst, me), send_sem=send_sem,
                recv_sem=recv_sem, device_id=(px, py, gz), device_id_type=MESH,
            ).start()
            return carry

        return send

    lax.fori_loop(1, tiles, send_keys, 0)
    pltpu.make_async_copy(key_out.at[me], key_in.at[me], key_recv).start()
    lax.fori_loop(1, tiles, sender(out_buf, in_buf, pay_send, pay_recv), 0)
    pltpu.make_async_copy(block(out_buf, me), block(in_buf, me), pay_recv).start()

    row, col = iota((points, points), 0), iota((points, points), 1)
    perm[...] = one_hot((row % ty) * tz + row // ty == col)
    load_v.wait()

    def reorder(c, carry):
        ordered = dot(perm[...], v[c]).astype(BF16)
        vp[c] = ordered
        vtp[c] = ordered.T
        return carry

    lax.fori_loop(0, tx, reorder, 0)

    pltpu.make_async_copy(key_in, key_in, key_recv).wait()
    row, lane = iota((128, orb), 0), iota((128, orb), 1)
    wanted = jnp.where((row & 7) == (lane & 7), lane // 8 + 1, -1).astype(F32)

    def place(i, carry):
        keys = key_in[pl.ds(i * 8, 8)]
        keys = jnp.broadcast_to(keys[:, :, None, :], (8, 2, 8, 128)).reshape(128, 128)
        hot = one_hot(jnp.concatenate([keys] * (orb // 128), axis=1) == wanted)
        at = pl.ds(pl.multiple_of(i * 128, 128), 128)
        hot_in[at, :] = hot
        hot_in_t[:, at] = hot.T
        hot_out_t[:, at] = hot_out[at, :].T
        return carry

    lax.fori_loop(0, tiles // 8, place, 0)

    pltpu.make_async_copy(in_buf, in_buf, pay_recv).wait()
    tmat[...] = dot(hot_in_t[...], in_buf[...]).astype(BF16)

    inner = ty * RADIUS

    def density(c, carry):
        values = vtp[c]
        mixed = dot(tmat[...], values)
        total = jnp.sum(mixed * values.astype(F32), axis=0, keepdims=True)
        halo[1, pl.ds(RADIUS + c, 1), pl.ds(inner, points)] = total
        return carry

    lax.fori_loop(0, tx, density, 0)

    row_ends = {0: ((RADIUS, tx), RADIUS), 1: ((tx, RADIUS), 0), -1: ((RADIUS, RADIUS), RADIUS + tx)}
    lane_ends = {0: ((inner, points), inner), 1: ((points, inner), 0), -1: ((inner, inner), inner + points)}
    copies = []
    for k, d in enumerate(neighbours):
        (r0, rn), r1 = row_ends[d[0]]
        (l0, ln), l1 = lane_ends[d[2]]
        copies.append(
            pltpu.make_async_remote_copy(
                src_ref=halo.at[1, pl.ds(r0, rn), pl.ds(l0, ln)],
                dst_ref=halo.at[1 - d[1], pl.ds(r1, rn), pl.ds(l1, ln)],
                send_sem=halo_send.at[k], recv_sem=halo_recv.at[k],
                device_id=near(d), device_id_type=MESH,
            )
        )
        copies[-1].start()
    for copy in copies:
        copy.wait_recv()

    for k, (cut, at) in enumerate((((ty - RADIUS, ty), 0), ((0, ty), RADIUS), ((0, RADIUS), RADIUS + ty))):
        high, low = split(halo[k])
        stacked = jnp.concatenate([high, low, high], axis=0)
        done = dot(stacked, xmat_ref[...], 0, 0).reshape(tz + 2 * RADIUS, ty, 128)
        fx[:, at : at + cut[1] - cut[0], :] = done[:, cut[0] : cut[1], :]

    def tap(s):
        return taps_ref[s : s + 1, :]

    for k in range((ty + 2 * RADIUS) // 8):
        at = pl.ds(8 * k, 8)
        total = tap(0) * fx[pl.ds(RADIUS, tz), at, :]
        for s in range(1, RADIUS + 1):
            total += tap(s) * (fx[pl.ds(RADIUS - s, tz), at, :] + fx[pl.ds(RADIUS + s, tz), at, :])
        fz[:, at, :] = total
    total = tap(16) * fz[:, pl.ds(RADIUS, ty), :]
    for s in range(1, RADIUS + 1):
        total += tap(16 + s) * (fz[:, pl.ds(RADIUS - s, ty), :] + fz[:, pl.ds(RADIUS + s, ty), :])
    both = jnp.concatenate(split(total.reshape(points, 128)), axis=1)
    gather = one_hot((iota((tx, 256), 1) & (tx - 1)) == iota((tx, 256), 0))
    pot[...] = dot(gather, both, 1, 1)

    weight = float(tx * points) ** (-0.5)
    acc[...] = jnp.zeros_like(acc)

    def gram(c, carry):
        scaled = pot[pl.ds(c, 1), :] * weight
        weighted = (vtp[c].astype(F32) * scaled).astype(BF16)
        acc[...] += dot(weighted, vp[c])
        return carry

    lax.fori_loop(0, tx, gram, 0)
    tmat[...] = acc[...].astype(BF16)

    def repack(i, carry):
        at = pl.ds(pl.multiple_of(i * rows, rows), rows)
        ret_buf[at, :] = dot(hot_in[at, :], tmat[...], 1, 1).astype(BF16)
        return carry

    lax.fori_loop(0, tiles * 16 // rows, repack, 0)
    lax.fori_loop(1, tiles, sender(ret_buf, back_buf, ret_send, ret_recv), 0)
    pltpu.make_async_copy(block(ret_buf, me), block(back_buf, me), ret_recv).start()

    high, rest = split(pot[...])
    rest = pot[...] - high.astype(F32)
    mid, low = split(rest)
    natural = dot(high, perm[...]) + (dot(mid, perm[...]) + dot(low, perm[...]))
    for y in range(ty):
        pot_ref[:, y, :] = natural[:, y * tz : (y + 1) * tz]

    for copy in copies:
        copy.wait_send()
    sent = key_out.at[pl.ds(0, tiles - 1)]
    pltpu.make_async_copy(sent, sent, key_send).wait()
    sent = out_buf.at[pl.ds(0, (tiles - 1) * 16), :]
    pltpu.make_async_copy(sent, sent, pay_send).wait()
    pltpu.make_async_copy(back_buf, back_buf, ret_recv).wait()
    own_ref[...] = dot(hot_out_t[...], back_buf[...]).astype(BF16)
    sent = ret_buf.at[pl.ds(0, (tiles - 1) * 16), :]
    pltpu.make_async_copy(sent, sent, ret_send).wait()


def solution(mesh):
    sizes = tuple(mesh.shape[a] for a in ("gx", "gy", "gz"))

    def local(values, slabs, slab_tile, slab_place):
        tx, ty, tz, orb = values.shape
        count = slabs.shape[0]
        points, tiles = ty * tz, sizes[0] * sizes[1]
        along_x, lanes = filter_tables(tx)
        high = along_x.astype(jnp.bfloat16)
        low = (along_x - high.astype(np.float32)).astype(jnp.bfloat16)
        xmat = np.concatenate([high, high, low], axis=0)
        wide = points + 2 * RADIUS * ty
        vm, any_ = pl.BlockSpec(memory_space=pltpu.VMEM), pl.BlockSpec(memory_space=pl.ANY)
        dma, slots = pltpu.SemaphoreType.DMA, tiles * 16
        pot, own = pl.pallas_call(
            functools.partial(kernel, (sizes, (tx, ty, tz), count, orb)),
            out_shape=(
                jax.ShapeDtypeStruct((tx, ty, tz), F32),
                jax.ShapeDtypeStruct((count * 8, orb), BF16),
            ),
            in_specs=[any_, any_, vm, vm, vm, vm],
            out_specs=(vm, vm),
            scratch_shapes=[
                pltpu.VMEM((tx, points, orb), BF16),
                pltpu.VMEM((count * 8, orb), BF16),
                pltpu.VMEM((tx, points, orb), BF16),
                pltpu.VMEM((tx, orb, points), BF16),
                pltpu.VMEM((points, points), BF16),
                pltpu.VMEM((slots, orb), BF16),
                pltpu.VMEM((orb, slots), BF16),
                pltpu.VMEM((slots, orb), BF16),
                pltpu.VMEM((orb, slots), BF16),
                pltpu.VMEM((tiles, 2, 128), F32),
                pltpu.VMEM((tiles, 2, 128), F32),
                pltpu.VMEM((slots, orb), BF16),
                pltpu.VMEM((slots, orb), BF16),
                pltpu.VMEM((slots, orb), BF16),
                pltpu.VMEM((slots, orb), BF16),
                pltpu.VMEM((orb, orb), BF16),
                pltpu.VMEM((orb, orb), F32),
                pltpu.VMEM((3, tx + 2 * RADIUS, wide), F32),
                pltpu.VMEM((tz + 2 * RADIUS, ty + 2 * RADIUS, 128), F32),
                pltpu.VMEM((tz, ty + 2 * RADIUS, 128), F32),
                pltpu.VMEM((tx, points), F32),
                dma((2,)), dma, dma, dma, dma, dma, dma, dma((26,)), dma((26,)),
            ],
            compiler_params=pltpu.CompilerParams(
                collective_id=0, has_side_effects=True, vmem_limit_bytes=56 * 1024 * 1024
            ),
        )(
            values.reshape(tx, points, orb),
            slabs.reshape(count * 8, orb),
            slab_tile.reshape(1, count),
            slab_place.reshape(1, count),
            jnp.asarray(xmat),
            jnp.asarray(lanes),
        )
        return pot, own.reshape(count, 8, orb)

    return jax.shard_map(
        local,
        mesh=mesh,
        in_specs=(
            P("gx", "gy", "gz", None),
            P(("gx", "gy", "gz"), None, None),
            P(("gx", "gy", "gz")),
            P(("gx", "gy", "gz")),
        ),
        out_specs=(P("gx", "gy", "gz"), P(("gx", "gy", "gz"), None, None)),
        check_vma=False,
    )
```

```python
import functools
import math

import jax
import jax.numpy as jnp
import numpy as np
from jax import lax
from jax.experimental import pallas as pl
from jax.experimental.pallas import tpu as pltpu
from jax.sharding import PartitionSpec as P

MESH = pl.DeviceIdType.MESH
RADIUS = 8
ALPHAS = (0.012, 0.025, 0.05, 0.1, 0.2, 0.4, 0.8, 1.6)
MIXES = (0.30, 0.30, 0.32, 0.34, 0.36, 0.38, 0.40, 0.42)
TERMS = len(ALPHAS)
F32 = jnp.float32
BF16 = jnp.bfloat16
I32 = jnp.int32


def filter_tables(tx):
    taps = np.array([[math.exp(-a * s * s) for s in range(RADIUS + 1)] for a in ALPHAS])
    norm = taps[:, 0] ** 2 + 2 * (taps[:, 1:] ** 2).sum(axis=1)
    mix = np.array(MIXES) / norm**1.5
    along_x = np.zeros((tx + 2 * RADIUS, TERMS, tx))
    for x in range(tx):
        for s in range(-RADIUS, RADIUS + 1):
            along_x[x + RADIUS + s, :, x] = taps[:, abs(s)]
    along_x = along_x.reshape(tx + 2 * RADIUS, TERMS * tx).astype(np.float32)
    lanes = np.zeros((32, TERMS * tx), np.float32)
    lanes[: RADIUS + 1] = np.repeat(taps, tx, axis=0).T
    lanes[16 : 16 + RADIUS + 1] = np.repeat(taps * mix[:, None], tx, axis=0).T
    return along_x, lanes


def iota(shape, dim):
    return lax.broadcasted_iota(I32, shape, dim)


def one_hot(mask):
    return jnp.where(mask, 1.0, 0.0).astype(BF16)


def split(a):
    high = a.astype(BF16)
    return high, (a - high.astype(F32)).astype(BF16)


def dot(a, b, ca=1, cb=0):
    return lax.dot_general(a, b, (((ca,), (cb,)), ((), ())), preferred_element_type=F32)


def kernel(
    dims,
    v_hbm, dm_hbm, tile_ref, place_ref, xmat_ref, taps_ref,
    pot_ref, own_ref,
    v, dm, vp, vtp, perm, hot_out, hot_out_t, hot_in, hot_in_t,
    key_out, key_in, out_buf, in_buf, ret_buf, back_buf,
    tmat, acc, halo, fx, fz, pot,
    local_sem, key_send, key_recv, pay_send, pay_recv,
    ret_send, ret_recv, halo_send, halo_recv,
):
    (nx, ny, nz), (tx, ty, tz), count, orb = dims
    tiles = nx * ny
    points = ty * tz
    gx, gy, gz = lax.axis_index("gx"), lax.axis_index("gy"), lax.axis_index("gz")
    me = gx * ny + gy

    def peer(step):
        back = tiles - step
        px = lax.rem(gx + back // ny, nx)
        py = lax.rem(gy + lax.rem(back, ny), ny)
        return px, py, px * ny + py

    def near(d):
        return tuple(
            lax.rem(at + by + size, size) for at, by, size in zip((gx, gy, gz), d, (nx, ny, nz))
        )

    neighbours = [
        (dx, dy, dz)
        for dz in (1, -1, 0)
        for dx in (1, -1, 0)
        for dy in (1, -1, 0)
        if (dx, dy, dz) != (0, 0, 0)
    ]
    others = [d for d in neighbours if d[2] != 0]

    load_dm = pltpu.make_async_copy(dm_hbm, dm, local_sem.at[0])
    load_dm.start()
    load_v = pltpu.make_async_copy(v_hbm, v, local_sem.at[1])
    load_v.start()
    barrier = pltpu.get_barrier_semaphore()

    def greet(step, carry):
        px, py, _ = peer(step)
        pl.semaphore_signal(barrier, inc=1, device_id=(px, py, gz), device_id_type=MESH)
        return carry

    lax.fori_loop(1, tiles, greet, 0)
    for d in others:
        pl.semaphore_signal(barrier, inc=1, device_id=near(d), device_id_type=MESH)

    owners = tile_ref[...]
    places = place_ref[...].astype(F32) + 1.0
    mine = one_hot(iota((tiles, count), 0) == owners)
    before = one_hot(iota((count, count), 0) < iota((count, count), 1))
    rank = jnp.sum(dot(mine, before) * mine.astype(F32), axis=0, keepdims=True)
    slot = 2.0 * owners.astype(F32) + rank
    spread = one_hot(iota((count, orb), 1) // 8 == iota((count, orb), 0))
    wide = dot(jnp.broadcast_to(slot, (8, count)).astype(BF16), spread)[0:1]
    slot_row = (wide * 8.0).astype(I32) + (iota((1, orb), 1) & 7)
    listed = [
        jnp.where(iota((tiles, count), 0) * 2 + s == slot.astype(I32), places, 0.0).astype(BF16)
        for s in range(2)
    ]
    key_out[:, 0, :] = sum(
        dot(listed[s], one_hot(iota((count, 128), 1) == 64 * s)) for s in range(2)
    )
    load_dm.wait()
    rows = 256

    def pack(i, carry):
        at = pl.ds(pl.multiple_of(i * rows, rows), rows)
        hot = one_hot(iota((rows, orb), 0) + i * rows == slot_row)
        hot_out[at, :] = hot
        out_buf[at, :] = dot(hot, dm[...]).astype(BF16)
        return carry

    lax.fori_loop(0, tiles * 16 // rows, pack, 0, unroll=True)

    pl.semaphore_wait(barrier, tiles - 1 + len(others))

    def block(ref, at):
        return ref.at[pl.ds(pl.multiple_of(at * 16, 16), 16), :]

    def send_keys(step, carry):
        px, py, at = peer(step)
        pltpu.make_async_remote_copy(
            src_ref=key_out.at[at], dst_ref=key_in.at[me], send_sem=key_send, recv_sem=key_recv,
            device_id=(px, py, gz), device_id_type=MESH,
        ).start()
        return carry

    def sender(src, dst, send_sem, recv_sem):
        def send(step, carry):
            px, py, at = peer(step)
            pltpu.make_async_remote_copy(
                src_ref=block(src, at), dst_ref=block(dst, me), send_sem=send_sem,
                recv_sem=recv_sem, device_id=(px, py, gz), device_id_type=MESH,
            ).start()
            return carry

        return send

    lax.fori_loop(1, tiles, send_keys, 0)
    pltpu.make_async_copy(key_out.at[me], key_in.at[me], key_recv).start()
    lax.fori_loop(1, tiles, sender(out_buf, in_buf, pay_send, pay_recv), 0)
    pltpu.make_async_copy(block(out_buf, me), block(in_buf, me), pay_recv).start()

    row, col = iota((points, points), 0), iota((points, points), 1)
    perm[...] = one_hot((row % ty) * tz + row // ty == col)
    load_v.wait()

    def reorder(c, carry):
        ordered = dot(perm[...], v[c]).astype(BF16)
        vp[c] = ordered
        vtp[c] = ordered.T
        return carry

    lax.fori_loop(0, tx, reorder, 0, unroll=4)

    pltpu.make_async_copy(key_in, key_in, key_recv).wait()
    row, lane = iota((128, orb), 0), iota((128, orb), 1)
    ours = (iota((128, 128), 1) // 64) == ((iota((128, 128), 0) // 8) & 1)
    wanted = jnp.where((row & 7) == (lane & 7), lane // 8 + 1, -1).astype(F32)

    def place(i, carry):
        keys = key_in[pl.ds(i * 8, 8)]
        keys = jnp.broadcast_to(keys, (8, 16, 128)).reshape(128, 128)
        keys = dot(jnp.where(ours, keys, 0.0).astype(BF16), jnp.ones((128, 128), BF16))
        hot = one_hot(jnp.concatenate([keys] * (orb // 128), axis=1) == wanted)
        at = pl.ds(pl.multiple_of(i * 128, 128), 128)
        hot_in[at, :] = hot
        hot_in_t[:, at] = hot.T
        hot_out_t[:, at] = hot_out[at, :].T
        return carry

    lax.fori_loop(0, tiles // 8, place, 0, unroll=2)

    pltpu.make_async_copy(in_buf, in_buf, pay_recv).wait()
    tmat[...] = dot(hot_in_t[...], in_buf[...]).astype(BF16)

    inner = ty * RADIUS

    def density(c, carry):
        values = vtp[c]
        mixed = dot(tmat[...], values)
        total = jnp.sum(mixed * values.astype(F32), axis=0, keepdims=True)
        halo[1, pl.ds(RADIUS + c, 1), pl.ds(inner, points)] = total
        return carry

    lax.fori_loop(0, tx, density, 0, unroll=True)

    row_ends = {0: ((RADIUS, tx), RADIUS), 1: ((tx, RADIUS), 0), -1: ((RADIUS, RADIUS), RADIUS + tx)}
    lane_ends = {0: ((inner, points), inner), 1: ((points, inner), 0), -1: ((inner, inner), inner + points)}
    copies = []
    for k, d in enumerate(neighbours):
        (r0, rn), r1 = row_ends[d[0]]
        (l0, ln), l1 = lane_ends[d[2]]
        copies.append(
            pltpu.make_async_remote_copy(
                src_ref=halo.at[1, pl.ds(r0, rn), pl.ds(l0, ln)],
                dst_ref=halo.at[1 - d[1], pl.ds(r1, rn), pl.ds(l1, ln)],
                send_sem=halo_send.at[k], recv_sem=halo_recv.at[k],
                device_id=near(d), device_id_type=MESH,
            )
        )
        copies[-1].start()
    for copy in copies:
        copy.wait_recv()

    for k, (cut, at) in enumerate((((ty - RADIUS, ty), 0), ((0, ty), RADIUS), ((0, RADIUS), RADIUS + ty))):
        high, low = split(halo[k])
        stacked = jnp.concatenate([high, low, high], axis=0)
        done = dot(stacked, xmat_ref[...], 0, 0).reshape(tz + 2 * RADIUS, ty, 128)
        fx[:, at : at + cut[1] - cut[0], :] = done[:, cut[0] : cut[1], :]

    def tap(s):
        return taps_ref[s : s + 1, :]

    for k in range((ty + 2 * RADIUS) // 8):
        at = pl.ds(8 * k, 8)
        total = tap(0) * fx[pl.ds(RADIUS, tz), at, :]
        for s in range(1, RADIUS + 1):
            total += tap(s) * (fx[pl.ds(RADIUS - s, tz), at, :] + fx[pl.ds(RADIUS + s, tz), at, :])
        fz[:, at, :] = total
    total = tap(16) * fz[:, pl.ds(RADIUS, ty), :]
    for s in range(1, RADIUS + 1):
        total += tap(16 + s) * (fz[:, pl.ds(RADIUS - s, ty), :] + fz[:, pl.ds(RADIUS + s, ty), :])
    both = jnp.concatenate(split(total.reshape(points, 128)), axis=1)
    gather = one_hot((iota((tx, 256), 1) & (tx - 1)) == iota((tx, 256), 0))
    pot[...] = dot(gather, both, 1, 1)

    weight = float(tx * points) ** (-0.5)
    acc[...] = jnp.zeros_like(acc)

    for c in range(0, tx, 4):
        weighted = [
            (vtp[k].astype(F32) * (pot[k : k + 1, :] * weight)).astype(BF16) for k in range(c, c + 4)
        ]
        acc[...] += dot(jnp.concatenate(weighted, axis=1), vp[c : c + 4].reshape(4 * points, orb))
    tmat[...] = acc[...].astype(BF16)

    def repack(i, carry):
        at = pl.ds(pl.multiple_of(i * rows, rows), rows)
        ret_buf[at, :] = dot(hot_in[at, :], tmat[...], 1, 1).astype(BF16)
        return carry

    lax.fori_loop(0, tiles * 16 // rows, repack, 0, unroll=True)
    lax.fori_loop(1, tiles, sender(ret_buf, back_buf, ret_send, ret_recv), 0)
    pltpu.make_async_copy(block(ret_buf, me), block(back_buf, me), ret_recv).start()

    high, rest = split(pot[...])
    rest = pot[...] - high.astype(F32)
    mid, low = split(rest)
    natural = dot(high, perm[...]) + (dot(mid, perm[...]) + dot(low, perm[...]))
    for y in range(ty):
        pot_ref[:, y, :] = natural[:, y * tz : (y + 1) * tz]

    for copy in copies:
        copy.wait_send()
    sent = key_out.at[pl.ds(0, tiles - 1)]
    pltpu.make_async_copy(sent, sent, key_send).wait()
    sent = out_buf.at[pl.ds(0, (tiles - 1) * 16), :]
    pltpu.make_async_copy(sent, sent, pay_send).wait()
    pltpu.make_async_copy(back_buf, back_buf, ret_recv).wait()
    own_ref[...] = dot(hot_out_t[...], back_buf[...]).astype(BF16)
    sent = ret_buf.at[pl.ds(0, (tiles - 1) * 16), :]
    pltpu.make_async_copy(sent, sent, ret_send).wait()


def hand_over(pot_ref, own_ref, pot_out, own_out, sem):
    copies = [
        pltpu.make_async_copy(pot_ref, pot_out, sem.at[0]),
        pltpu.make_async_copy(own_ref, own_out, sem.at[1]),
    ]
    for copy in copies:
        copy.start()
    for copy in copies:
        copy.wait()


def solution(mesh):
    sizes = tuple(mesh.shape[a] for a in ("gx", "gy", "gz"))

    def local(values, slabs, slab_tile, slab_place):
        tx, ty, tz, orb = values.shape
        count = slabs.shape[0]
        points, tiles = ty * tz, sizes[0] * sizes[1]
        along_x, lanes = filter_tables(tx)
        high = along_x.astype(jnp.bfloat16)
        low = (along_x - high.astype(np.float32)).astype(jnp.bfloat16)
        xmat = np.concatenate([high, high, low], axis=0)
        wide = points + 2 * RADIUS * ty
        vm, any_ = pl.BlockSpec(memory_space=pltpu.VMEM), pl.BlockSpec(memory_space=pl.ANY)
        dma, slots = pltpu.SemaphoreType.DMA, tiles * 16
        pot, own = pl.pallas_call(
            functools.partial(kernel, (sizes, (tx, ty, tz), count, orb)),
            out_shape=(
                jax.ShapeDtypeStruct((tx, ty, tz), F32),
                jax.ShapeDtypeStruct((count * 8, orb), BF16),
            ),
            in_specs=[any_, any_, vm, vm, vm, vm],
            out_specs=(vm, vm),
            scratch_shapes=[
                pltpu.VMEM((tx, points, orb), BF16),
                pltpu.VMEM((count * 8, orb), BF16),
                pltpu.VMEM((tx, points, orb), BF16),
                pltpu.VMEM((tx, orb, points), BF16),
                pltpu.VMEM((points, points), BF16),
                pltpu.VMEM((slots, orb), BF16),
                pltpu.VMEM((orb, slots), BF16),
                pltpu.VMEM((slots, orb), BF16),
                pltpu.VMEM((orb, slots), BF16),
                pltpu.VMEM((tiles, 1, 128), F32),
                pltpu.VMEM((tiles, 1, 128), F32),
                pltpu.VMEM((slots, orb), BF16),
                pltpu.VMEM((slots, orb), BF16),
                pltpu.VMEM((slots, orb), BF16),
                pltpu.VMEM((slots, orb), BF16),
                pltpu.VMEM((orb, orb), BF16),
                pltpu.VMEM((orb, orb), F32),
                pltpu.VMEM((3, tx + 2 * RADIUS, wide), F32),
                pltpu.VMEM((tz + 2 * RADIUS, ty + 2 * RADIUS, 128), F32),
                pltpu.VMEM((tz, ty + 2 * RADIUS, 128), F32),
                pltpu.VMEM((tx, points), F32),
                dma((2,)), dma, dma, dma, dma, dma, dma, dma((26,)), dma((26,)),
            ],
            compiler_params=pltpu.CompilerParams(
                collective_id=0, has_side_effects=True, vmem_limit_bytes=56 * 1024 * 1024
            ),
        )(
            values.reshape(tx, points, orb),
            slabs.reshape(count * 8, orb),
            slab_tile.reshape(1, count),
            slab_place.reshape(1, count),
            jnp.asarray(xmat),
            jnp.asarray(lanes),
        )
        pot, own = pl.pallas_call(
            hand_over,
            out_shape=(
                jax.ShapeDtypeStruct((tx, ty, tz), F32),
                jax.ShapeDtypeStruct((count * 8, orb), BF16),
            ),
            in_specs=[any_, any_],
            out_specs=(any_, any_),
            scratch_shapes=[dma((2,))],
        )(pot, own)
        return pot, own.reshape(count, 8, orb)

    return jax.shard_map(
        local,
        mesh=mesh,
        in_specs=(
            P("gx", "gy", "gz", None),
            P(("gx", "gy", "gz"), None, None),
            P(("gx", "gy", "gz")),
            P(("gx", "gy", "gz")),
        ),
        out_specs=(P("gx", "gy", "gz"), P(("gx", "gy", "gz"), None, None)),
        check_vma=False,
    )
```

```python
import functools
import math

import jax
import jax.numpy as jnp
import numpy as np
from jax import lax
from jax.experimental import pallas as pl
from jax.experimental.pallas import tpu as pltpu
from jax.sharding import PartitionSpec as P

MESH = pl.DeviceIdType.MESH
RADIUS = 8
ALPHAS = (0.012, 0.025, 0.05, 0.1, 0.2, 0.4, 0.8, 1.6)
MIXES = (0.30, 0.30, 0.32, 0.34, 0.36, 0.38, 0.40, 0.42)
TERMS = len(ALPHAS)
F32 = jnp.float32
BF16 = jnp.bfloat16
I32 = jnp.int32


def filter_tables(tx):
    taps = np.array([[math.exp(-a * s * s) for s in range(RADIUS + 1)] for a in ALPHAS])
    norm = taps[:, 0] ** 2 + 2 * (taps[:, 1:] ** 2).sum(axis=1)
    mix = np.array(MIXES) / norm**1.5
    along_x = np.zeros((tx + 2 * RADIUS, TERMS, tx))
    for x in range(tx):
        for s in range(-RADIUS, RADIUS + 1):
            along_x[x + RADIUS + s, :, x] = taps[:, abs(s)]
    along_x = along_x.reshape(tx + 2 * RADIUS, TERMS * tx).astype(np.float32)
    lanes = np.zeros((32, TERMS * tx), np.float32)
    lanes[: RADIUS + 1] = np.repeat(taps, tx, axis=0).T
    lanes[16 : 16 + RADIUS + 1] = np.repeat(taps * mix[:, None], tx, axis=0).T
    return along_x, lanes


def iota(shape, dim):
    return lax.broadcasted_iota(I32, shape, dim)


def one_hot(mask):
    return jnp.where(mask, 1.0, 0.0).astype(BF16)


def split(a):
    high = a.astype(BF16)
    return high, (a - high.astype(F32)).astype(BF16)


def dot(a, b, ca=1, cb=0):
    return lax.dot_general(a, b, (((ca,), (cb,)), ((), ())), preferred_element_type=F32)


def kernel(
    dims,
    v_hbm, dm_hbm, tile_hbm, place_hbm, xmat_hbm, taps_hbm,
    pot_ref, own_ref,
    v, dm, vp, vtp, perm, hot_out, hot_out_t, hot_in, hot_in_t,
    key_out, key_in, out_buf, in_buf, ret_buf, back_buf,
    tmat, acc, halo, fx, fz, pot,
    tile_ref, place_ref, xmat_ref, taps_ref, local_sem, key_send, key_recv, pay_send, pay_recv,
    ret_send, ret_recv, halo_send, halo_recv,
):
    (nx, ny, nz), (tx, ty, tz), count, orb = dims
    tiles = nx * ny
    points = ty * tz
    gx, gy, gz = lax.axis_index("gx"), lax.axis_index("gy"), lax.axis_index("gz")
    me = gx * ny + gy

    def peer(step):
        back = tiles - step
        px = lax.rem(gx + back // ny, nx)
        py = lax.rem(gy + lax.rem(back, ny), ny)
        return px, py, px * ny + py

    def near(d):
        return tuple(
            lax.rem(at + by + size, size) for at, by, size in zip((gx, gy, gz), d, (nx, ny, nz))
        )

    neighbours = [
        (dx, dy, dz)
        for dz in (1, -1, 0)
        for dx in (1, -1, 0)
        for dy in (1, -1, 0)
        if (dx, dy, dz) != (0, 0, 0)
    ]
    others = [d for d in neighbours if d[2] != 0]

    loads = [
        pltpu.make_async_copy(*pair, local_sem.at[k])
        for k, pair in enumerate((
            (tile_hbm, tile_ref), (place_hbm, place_ref), (dm_hbm, dm),
            (v_hbm, v), (xmat_hbm, xmat_ref), (taps_hbm, taps_ref),
        ))
    ]
    for load in loads:
        load.start()
    barrier = pltpu.get_barrier_semaphore()

    def greet(step, carry):
        px, py, _ = peer(step)
        pl.semaphore_signal(barrier, inc=1, device_id=(px, py, gz), device_id_type=MESH)
        return carry

    lax.fori_loop(1, tiles, greet, 0)
    for d in others:
        pl.semaphore_signal(barrier, inc=1, device_id=near(d), device_id_type=MESH)

    loads[0].wait()
    loads[1].wait()
    owners = tile_ref[...]
    places = place_ref[...].astype(F32) + 1.0
    mine = one_hot(iota((tiles, count), 0) == owners)
    before = one_hot(iota((count, count), 0) < iota((count, count), 1))
    rank = jnp.sum(dot(mine, before) * mine.astype(F32), axis=0, keepdims=True)
    slot = 2.0 * owners.astype(F32) + rank
    spread = one_hot(iota((count, orb), 1) // 8 == iota((count, orb), 0))
    wide = dot(jnp.broadcast_to(slot, (8, count)).astype(BF16), spread)[0:1]
    slot_row = (wide * 8.0).astype(I32) + (iota((1, orb), 1) & 7)
    listed = [
        jnp.where(iota((tiles, count), 0) * 2 + s == slot.astype(I32), places, 0.0).astype(BF16)
        for s in range(2)
    ]
    key_out[:, 0, :] = sum(
        dot(listed[s], one_hot(iota((count, 128), 1) == 64 * s)) for s in range(2)
    )
    loads[2].wait()
    rows = 256

    def pack(i, carry):
        at = pl.ds(pl.multiple_of(i * rows, rows), rows)
        hot = one_hot(iota((rows, orb), 0) + i * rows == slot_row)
        hot_out[at, :] = hot
        out_buf[at, :] = dot(hot, dm[...]).astype(BF16)
        return carry

    lax.fori_loop(0, tiles * 16 // rows, pack, 0, unroll=True)

    pl.semaphore_wait(barrier, tiles - 1 + len(others))

    def block(ref, at):
        return ref.at[pl.ds(pl.multiple_of(at * 16, 16), 16), :]

    def send_keys(step, carry):
        px, py, at = peer(step)
        pltpu.make_async_remote_copy(
            src_ref=key_out.at[at], dst_ref=key_in.at[me], send_sem=key_send, recv_sem=key_recv,
            device_id=(px, py, gz), device_id_type=MESH,
        ).start()
        return carry

    def sender(src, dst, send_sem, recv_sem):
        def send(step, carry):
            px, py, at = peer(step)
            pltpu.make_async_remote_copy(
                src_ref=block(src, at), dst_ref=block(dst, me), send_sem=send_sem,
                recv_sem=recv_sem.at[gx], device_id=(px, py, gz), device_id_type=MESH,
            ).start()
            return carry

        return send

    span = ny * 16

    def gathered(hot_t, buf, sem):
        acc[...] = jnp.zeros_like(acc)

        def add(step, carry):
            at = lax.rem(gx + step, nx)
            part = pl.ds(pl.multiple_of(at * span, span), span)
            pltpu.make_async_copy(buf.at[part, :], buf.at[part, :], sem.at[at]).wait()
            acc[...] += dot(hot_t[:, part], buf[part, :])
            return carry

        lax.fori_loop(1, nx + 1, add, 0)
        return acc[...].astype(BF16)

    lax.fori_loop(1, tiles, send_keys, 0)
    pltpu.make_async_copy(key_out.at[me], key_in.at[me], key_recv).start()
    lax.fori_loop(1, tiles, sender(out_buf, in_buf, pay_send, pay_recv), 0)
    pltpu.make_async_copy(block(out_buf, me), block(in_buf, me), pay_recv.at[gx]).start()

    row, col = iota((points, points), 0), iota((points, points), 1)
    perm[...] = one_hot((row % ty) * tz + row // ty == col)
    for load in loads[3:]:
        load.wait()

    def reorder(c, carry):
        ordered = dot(perm[...], v[c]).astype(BF16)
        vp[c] = ordered
        vtp[c] = ordered.T
        return carry

    lax.fori_loop(0, tx, reorder, 0, unroll=4)

    pltpu.make_async_copy(key_in, key_in, key_recv).wait()
    row, lane = iota((128, orb), 0), iota((128, orb), 1)
    ours = (iota((128, 128), 1) // 64) == ((iota((128, 128), 0) // 8) & 1)
    wanted = jnp.where((row & 7) == (lane & 7), lane // 8 + 1, -1).astype(F32)

    def place(i, carry):
        keys = key_in[pl.ds(i * 8, 8)]
        keys = jnp.broadcast_to(keys, (8, 16, 128)).reshape(128, 128)
        keys = dot(jnp.where(ours, keys, 0.0).astype(BF16), jnp.ones((128, 128), BF16))
        hot = one_hot(jnp.concatenate([keys] * (orb // 128), axis=1) == wanted)
        at = pl.ds(pl.multiple_of(i * 128, 128), 128)
        hot_in[at, :] = hot
        hot_in_t[:, at] = hot.T
        hot_out_t[:, at] = hot_out[at, :].T
        return carry

    lax.fori_loop(0, tiles // 8, place, 0, unroll=2)

    tmat[...] = gathered(hot_in_t, in_buf, pay_recv)

    inner = ty * RADIUS

    def density(c, carry):
        values = vtp[c]
        mixed = dot(tmat[...], values)
        total = jnp.sum(mixed * values.astype(F32), axis=0, keepdims=True)
        halo[1, pl.ds(RADIUS + c, 1), pl.ds(inner, points)] = total
        return carry

    lax.fori_loop(0, tx, density, 0, unroll=True)

    row_ends = {0: ((RADIUS, tx), RADIUS), 1: ((tx, RADIUS), 0), -1: ((RADIUS, RADIUS), RADIUS + tx)}
    lane_ends = {0: ((inner, points), inner), 1: ((points, inner), 0), -1: ((inner, inner), inner + points)}
    copies = []
    for k, d in enumerate(neighbours):
        (r0, rn), r1 = row_ends[d[0]]
        (l0, ln), l1 = lane_ends[d[2]]
        copies.append(
            pltpu.make_async_remote_copy(
                src_ref=halo.at[1, pl.ds(r0, rn), pl.ds(l0, ln)],
                dst_ref=halo.at[1 - d[1], pl.ds(r1, rn), pl.ds(l1, ln)],
                send_sem=halo_send.at[k], recv_sem=halo_recv.at[k],
                device_id=near(d), device_id_type=MESH,
            )
        )
        copies[-1].start()
    for copy in copies:
        copy.wait_recv()

    for k, (cut, at) in enumerate((((ty - RADIUS, ty), 0), ((0, ty), RADIUS), ((0, RADIUS), RADIUS + ty))):
        high, low = split(halo[k])
        stacked = jnp.concatenate([high, low, high], axis=0)
        done = dot(stacked, xmat_ref[...], 0, 0).reshape(tz + 2 * RADIUS, ty, 128)
        fx[:, at : at + cut[1] - cut[0], :] = done[:, cut[0] : cut[1], :]

    def tap(s):
        return taps_ref[s : s + 1, :]

    for k in range((ty + 2 * RADIUS) // 8):
        at = pl.ds(8 * k, 8)
        total = tap(0) * fx[pl.ds(RADIUS, tz), at, :]
        for s in range(1, RADIUS + 1):
            total += tap(s) * (fx[pl.ds(RADIUS - s, tz), at, :] + fx[pl.ds(RADIUS + s, tz), at, :])
        fz[:, at, :] = total
    total = tap(16) * fz[:, pl.ds(RADIUS, ty), :]
    for s in range(1, RADIUS + 1):
        total += tap(16 + s) * (fz[:, pl.ds(RADIUS - s, ty), :] + fz[:, pl.ds(RADIUS + s, ty), :])
    both = jnp.concatenate(split(total.reshape(points, 128)), axis=1)
    gather = one_hot((iota((tx, 256), 1) & (tx - 1)) == iota((tx, 256), 0))
    pot[...] = dot(gather, both, 1, 1)

    weight = float(tx * points) ** (-0.5)
    acc[...] = jnp.zeros_like(acc)

    for c in range(0, tx, 4):
        weighted = [
            (vtp[k].astype(F32) * (pot[k : k + 1, :] * weight)).astype(BF16) for k in range(c, c + 4)
        ]
        acc[...] += dot(jnp.concatenate(weighted, axis=1), vp[c : c + 4].reshape(4 * points, orb))
    tmat[...] = acc[...].astype(BF16)

    def repack(i, carry):
        at = pl.ds(pl.multiple_of(i * rows, rows), rows)
        ret_buf[at, :] = dot(hot_in[at, :], tmat[...], 1, 1).astype(BF16)
        return carry

    lax.fori_loop(0, tiles * 16 // rows, repack, 0, unroll=True)
    lax.fori_loop(1, tiles, sender(ret_buf, back_buf, ret_send, ret_recv), 0)
    pltpu.make_async_copy(block(ret_buf, me), block(back_buf, me), ret_recv.at[gx]).start()

    high, rest = split(pot[...])
    rest = pot[...] - high.astype(F32)
    mid, low = split(rest)
    natural = dot(high, perm[...]) + (dot(mid, perm[...]) + dot(low, perm[...]))
    for y in range(ty):
        pot_ref[:, y, :] = natural[:, y * tz : (y + 1) * tz]

    for copy in copies:
        copy.wait_send()
    sent = key_out.at[pl.ds(0, tiles - 1)]
    pltpu.make_async_copy(sent, sent, key_send).wait()
    sent = out_buf.at[pl.ds(0, (tiles - 1) * 16), :]
    pltpu.make_async_copy(sent, sent, pay_send).wait()
    own_ref[...] = gathered(hot_out_t, back_buf, ret_recv)
    sent = ret_buf.at[pl.ds(0, (tiles - 1) * 16), :]
    pltpu.make_async_copy(sent, sent, ret_send).wait()


def hand_over(pot_ref, own_ref, pot_out, own_out):
    pot_out[...] = pot_ref[...]
    own_out[...] = own_ref[...]


def solution(mesh):
    sizes = tuple(mesh.shape[a] for a in ("gx", "gy", "gz"))

    def local(values, slabs, slab_tile, slab_place):
        tx, ty, tz, orb = values.shape
        count = slabs.shape[0]
        points, tiles = ty * tz, sizes[0] * sizes[1]
        along_x, lanes = filter_tables(tx)
        high = along_x.astype(jnp.bfloat16)
        low = (along_x - high.astype(np.float32)).astype(jnp.bfloat16)
        xmat = np.concatenate([high, high, low], axis=0)
        wide = points + 2 * RADIUS * ty
        vm, any_ = pl.BlockSpec(memory_space=pltpu.VMEM), pl.BlockSpec(memory_space=pl.ANY)
        dma, slots = pltpu.SemaphoreType.DMA, tiles * 16
        pot, own = pl.pallas_call(
            functools.partial(kernel, (sizes, (tx, ty, tz), count, orb)),
            out_shape=(
                jax.ShapeDtypeStruct((tx, ty, tz), F32),
                jax.ShapeDtypeStruct((count * 8, orb), BF16),
            ),
            in_specs=[any_] * 6,
            out_specs=(vm, vm),
            scratch_shapes=[
                pltpu.VMEM((tx, points, orb), BF16),
                pltpu.VMEM((count * 8, orb), BF16),
                pltpu.VMEM((tx, points, orb), BF16),
                pltpu.VMEM((tx, orb, points), BF16),
                pltpu.VMEM((points, points), BF16),
                pltpu.VMEM((slots, orb), BF16),
                pltpu.VMEM((orb, slots), BF16),
                pltpu.VMEM((slots, orb), BF16),
                pltpu.VMEM((orb, slots), BF16),
                pltpu.VMEM((tiles, 1, 128), F32),
                pltpu.VMEM((tiles, 1, 128), F32),
                pltpu.VMEM((slots, orb), BF16),
                pltpu.VMEM((slots, orb), BF16),
                pltpu.VMEM((slots, orb), BF16),
                pltpu.VMEM((slots, orb), BF16),
                pltpu.VMEM((orb, orb), BF16),
                pltpu.VMEM((orb, orb), F32),
                pltpu.VMEM((3, tx + 2 * RADIUS, wide), F32),
                pltpu.VMEM((tz + 2 * RADIUS, ty + 2 * RADIUS, 128), F32),
                pltpu.VMEM((tz, ty + 2 * RADIUS, 128), F32),
                pltpu.VMEM((tx, points), F32),
                pltpu.VMEM((1, count), I32),
                pltpu.VMEM((1, count), I32),
                pltpu.VMEM(xmat.shape, BF16),
                pltpu.VMEM(lanes.shape, F32),
                dma((6,)), dma, dma, dma, dma((sizes[0],)), dma, dma((sizes[0],)), dma((26,)), dma((26,)),
            ],
            compiler_params=pltpu.CompilerParams(
                collective_id=0, has_side_effects=True, vmem_limit_bytes=56 * 1024 * 1024
            ),
        )(
            values.reshape(tx, points, orb),
            slabs.reshape(count * 8, orb),
            slab_tile.reshape(1, count),
            slab_place.reshape(1, count),
            jnp.asarray(xmat),
            jnp.asarray(lanes),
        )
        pot, own = pl.pallas_call(
            hand_over,
            out_shape=(
                jax.ShapeDtypeStruct((tx, ty, tz), F32),
                jax.ShapeDtypeStruct((count * 8, orb), BF16),
            ),
            in_specs=[vm, vm],
            out_specs=(vm, vm),
        )(pot, own)
        return pot, own.reshape(count, 8, orb)

    return jax.shard_map(
        local,
        mesh=mesh,
        in_specs=(
            P("gx", "gy", "gz", None),
            P(("gx", "gy", "gz"), None, None),
            P(("gx", "gy", "gz")),
            P(("gx", "gy", "gz")),
        ),
        out_specs=(P("gx", "gy", "gz"), P(("gx", "gy", "gz"), None, None)),
        check_vma=False,
    )
```

```python
import functools
import math

import jax
import jax.numpy as jnp
import numpy as np
from jax import lax
from jax.experimental import pallas as pl
from jax.experimental.pallas import tpu as pltpu
from jax.sharding import PartitionSpec as P

MESH = pl.DeviceIdType.MESH
RADIUS = 8
ALPHAS = (0.012, 0.025, 0.05, 0.1, 0.2, 0.4, 0.8, 1.6)
MIXES = (0.30, 0.30, 0.32, 0.34, 0.36, 0.38, 0.40, 0.42)
TERMS = len(ALPHAS)
F32 = jnp.float32
BF16 = jnp.bfloat16
I32 = jnp.int32


def filter_tables(tx):
    taps = np.array([[math.exp(-a * s * s) for s in range(RADIUS + 1)] for a in ALPHAS])
    norm = taps[:, 0] ** 2 + 2 * (taps[:, 1:] ** 2).sum(axis=1)
    mix = np.array(MIXES) / norm**1.5
    along_x = np.zeros((tx + 2 * RADIUS, TERMS, tx))
    for x in range(tx):
        for s in range(-RADIUS, RADIUS + 1):
            along_x[x + RADIUS + s, :, x] = taps[:, abs(s)]
    along_x = along_x.reshape(tx + 2 * RADIUS, TERMS * tx).astype(np.float32)
    lanes = np.zeros((32, TERMS * tx), np.float32)
    lanes[: RADIUS + 1] = np.repeat(taps, tx, axis=0).T
    lanes[16 : 16 + RADIUS + 1] = np.repeat(taps * mix[:, None], tx, axis=0).T
    return along_x, lanes


def iota(shape, dim):
    return lax.broadcasted_iota(I32, shape, dim)


def one_hot(mask):
    return jnp.where(mask, 1.0, 0.0).astype(BF16)


def split(a):
    high = a.astype(BF16)
    return high, (a - high.astype(F32)).astype(BF16)


def dot(a, b, ca=1, cb=0):
    return lax.dot_general(a, b, (((ca,), (cb,)), ((), ())), preferred_element_type=F32)


def kernel(
    dims,
    v_hbm, dm_hbm, tile_hbm, place_hbm, xmat_hbm, taps_hbm,
    pot_ref, own_ref,
    v, dm, vp, vtp, perm, hot_out, hot_out_t, hot_in, hot_in_t,
    key_out, key_in, out_buf, in_buf, ret_buf, back_buf,
    tmat, acc, halo, fx, fz, pot,
    tile_ref, place_ref, xmat_ref, taps_ref, local_sem, key_send, key_recv, pay_send, pay_recv,
    ret_send, ret_recv, halo_send, halo_recv,
):
    (nx, ny, nz), (tx, ty, tz), count, orb = dims
    tiles = nx * ny
    points = ty * tz
    gx, gy, gz = lax.axis_index("gx"), lax.axis_index("gy"), lax.axis_index("gz")
    me = gx * ny + gy

    def peer(step):
        back = tiles - step
        px = lax.rem(gx + back // ny, nx)
        py = lax.rem(gy + lax.rem(back, ny), ny)
        return px, py, px * ny + py

    def near(d):
        return tuple(
            lax.rem(at + by + size, size) for at, by, size in zip((gx, gy, gz), d, (nx, ny, nz))
        )

    neighbours = [
        (dx, dy, dz)
        for dz in (1, -1, 0)
        for dx in (1, -1, 0)
        for dy in (1, -1, 0)
        if (dx, dy, dz) != (0, 0, 0)
    ]
    others = [d for d in neighbours if d[2] != 0]

    loads = [
        pltpu.make_async_copy(*pair, local_sem.at[k])
        for k, pair in enumerate((
            (tile_hbm, tile_ref), (place_hbm, place_ref), (dm_hbm, dm),
            (v_hbm, v), (xmat_hbm, xmat_ref), (taps_hbm, taps_ref),
        ))
    ]
    for load in loads:
        load.start()
    barrier = pltpu.get_barrier_semaphore()

    def greet(step, carry):
        px, py, _ = peer(step)
        pl.semaphore_signal(barrier, inc=1, device_id=(px, py, gz), device_id_type=MESH)
        return carry

    lax.fori_loop(1, tiles, greet, 0)
    for d in others:
        pl.semaphore_signal(barrier, inc=1, device_id=near(d), device_id_type=MESH)

    loads[0].wait()
    loads[1].wait()
    owners = tile_ref[...]
    places = place_ref[...].astype(F32) + 1.0
    mine = one_hot(iota((tiles, count), 0) == owners)
    before = one_hot(iota((count, count), 0) < iota((count, count), 1))
    rank = jnp.sum(dot(mine, before) * mine.astype(F32), axis=0, keepdims=True)
    slot = 2.0 * owners.astype(F32) + rank
    spread = one_hot(iota((count, orb), 1) // 8 == iota((count, orb), 0))
    wide = dot(jnp.broadcast_to(slot, (8, count)).astype(BF16), spread)[0:1]
    slot_row = (wide * 8.0).astype(I32) + (iota((1, orb), 1) & 7)
    listed = [
        jnp.where(iota((tiles, count), 0) * 2 + s == slot.astype(I32), places, 0.0).astype(BF16)
        for s in range(2)
    ]
    key_out[:, 0, :] = sum(
        dot(listed[s], one_hot(iota((count, 128), 1) == 64 * s)) for s in range(2)
    )
    loads[2].wait()
    rows = 256

    def pack(i, carry):
        at = pl.ds(pl.multiple_of(i * rows, rows), rows)
        hot = one_hot(iota((rows, orb), 0) + i * rows == slot_row)
        hot_out[at, :] = hot
        out_buf[at, :] = dot(hot, dm[...]).astype(BF16)
        return carry

    lax.fori_loop(0, tiles * 16 // rows, pack, 0, unroll=True)

    pl.semaphore_wait(barrier, tiles - 1 + len(others))

    def block(ref, at, cols):
        return ref.at[pl.ds(pl.multiple_of(at * 16, 16), 16), pl.ds(cols[0], cols[1] - cols[0])]

    def send_keys(step, carry):
        px, py, at = peer(step)
        pltpu.make_async_remote_copy(
            src_ref=key_out.at[at], dst_ref=key_in.at[me], send_sem=key_send, recv_sem=key_recv,
            device_id=(px, py, gz), device_id_type=MESH,
        ).start()
        return carry

    def exchange(src, dst, send_sem, recv_sem, cols):
        def send(step, carry):
            px, py, at = peer(step)
            pltpu.make_async_remote_copy(
                src_ref=block(src, at, cols), dst_ref=block(dst, me, cols), send_sem=send_sem,
                recv_sem=recv_sem.at[gx], device_id=(px, py, gz), device_id_type=MESH,
            ).start()
            return carry

        lax.fori_loop(1, tiles, send, 0)
        pltpu.make_async_copy(block(src, me, cols), block(dst, me, cols), recv_sem.at[gx]).start()

    span = ny * 16

    def gathered(hot_t, buf, sem, cols):
        to = pl.ds(cols[0], cols[1] - cols[0])
        acc[:, to] = jnp.zeros_like(acc[:, to])

        def add(step, carry):
            at = lax.rem(gx + step, nx)
            part = pl.ds(pl.multiple_of(at * span, span), span)
            pltpu.make_async_copy(buf.at[part, to], buf.at[part, to], sem.at[at]).wait()
            acc[:, to] += dot(hot_t[:, part], buf[part, to])
            return carry

        lax.fori_loop(1, nx + 1, add, 0)
        return acc[:, to]

    lax.fori_loop(1, tiles, send_keys, 0)
    pltpu.make_async_copy(key_out.at[me], key_in.at[me], key_recv).start()
    there, home = ((0, 256), (256, orb)), ((0, 128), (128, orb))
    for k, cols in enumerate(there):
        exchange(out_buf, in_buf, pay_send, pay_recv.at[k], cols)

    row, col = iota((points, points), 0), iota((points, points), 1)
    perm[...] = one_hot((row % ty) * tz + row // ty == col)
    for load in loads[3:]:
        load.wait()

    def reorder(c, carry):
        ordered = dot(perm[...], v[c]).astype(BF16)
        vp[c] = ordered
        vtp[c] = ordered.T
        return carry

    lax.fori_loop(0, tx, reorder, 0, unroll=4)

    pltpu.make_async_copy(key_in, key_in, key_recv).wait()
    row, lane = iota((128, orb), 0), iota((128, orb), 1)
    ours = (iota((128, 128), 1) // 64) == ((iota((128, 128), 0) // 8) & 1)
    wanted = jnp.where((row & 7) == (lane & 7), lane // 8 + 1, -1).astype(F32)

    def place(i, carry):
        keys = key_in[pl.ds(i * 8, 8)]
        keys = jnp.broadcast_to(keys, (8, 16, 128)).reshape(128, 128)
        keys = dot(jnp.where(ours, keys, 0.0).astype(BF16), jnp.ones((128, 128), BF16))
        hot = one_hot(jnp.concatenate([keys] * (orb // 128), axis=1) == wanted)
        at = pl.ds(pl.multiple_of(i * 128, 128), 128)
        hot_in[at, :] = hot
        hot_in_t[:, at] = hot.T
        hot_out_t[:, at] = hot_out[at, :].T
        return carry

    lax.fori_loop(0, tiles // 8, place, 0, unroll=2)

    inner = ty * RADIUS
    for k, cols in enumerate(there):
        part = pl.ds(cols[0], cols[1] - cols[0])
        tmat[part, :] = gathered(hot_in_t, in_buf, pay_recv.at[k], cols).T.astype(BF16)

        def density(c, carry, k=k, part=part):
            mixed = dot(tmat[part, :], vtp[c])
            total = jnp.sum(mixed * vtp[c, part, :].astype(F32), axis=0, keepdims=True)
            at = halo.at[1, pl.ds(RADIUS + c, 1), pl.ds(inner, points)]
            at[...] = total if k == 0 else at[...] + total
            return carry

        lax.fori_loop(0, tx, density, 0, unroll=True)

    row_ends = {0: ((RADIUS, tx), RADIUS), 1: ((tx, RADIUS), 0), -1: ((RADIUS, RADIUS), RADIUS + tx)}
    lane_ends = {0: ((inner, points), inner), 1: ((points, inner), 0), -1: ((inner, inner), inner + points)}
    copies = []
    for k, d in enumerate(neighbours):
        (r0, rn), r1 = row_ends[d[0]]
        (l0, ln), l1 = lane_ends[d[2]]
        copies.append(
            pltpu.make_async_remote_copy(
                src_ref=halo.at[1, pl.ds(r0, rn), pl.ds(l0, ln)],
                dst_ref=halo.at[1 - d[1], pl.ds(r1, rn), pl.ds(l1, ln)],
                send_sem=halo_send.at[k], recv_sem=halo_recv.at[k],
                device_id=near(d), device_id_type=MESH,
            )
        )
        copies[-1].start()
    for copy in copies:
        copy.wait_recv()

    for k, (cut, at) in enumerate((((ty - RADIUS, ty), 0), ((0, ty), RADIUS), ((0, RADIUS), RADIUS + ty))):
        high, low = split(halo[k])
        stacked = jnp.concatenate([high, low, high], axis=0)
        done = dot(stacked, xmat_ref[...], 0, 0).reshape(tz + 2 * RADIUS, ty, 128)
        fx[:, at : at + cut[1] - cut[0], :] = done[:, cut[0] : cut[1], :]

    def tap(s):
        return taps_ref[s : s + 1, :]

    for k in range((ty + 2 * RADIUS) // 8):
        at = pl.ds(8 * k, 8)
        total = tap(0) * fx[pl.ds(RADIUS, tz), at, :]
        for s in range(1, RADIUS + 1):
            total += tap(s) * (fx[pl.ds(RADIUS - s, tz), at, :] + fx[pl.ds(RADIUS + s, tz), at, :])
        fz[:, at, :] = total
    total = tap(16) * fz[:, pl.ds(RADIUS, ty), :]
    for s in range(1, RADIUS + 1):
        total += tap(16 + s) * (fz[:, pl.ds(RADIUS - s, ty), :] + fz[:, pl.ds(RADIUS + s, ty), :])
    both = jnp.concatenate(split(total.reshape(points, 128)), axis=1)
    gather = one_hot((iota((tx, 256), 1) & (tx - 1)) == iota((tx, 256), 0))
    pot[...] = dot(gather, both, 1, 1)

    weight = float(tx * points) ** (-0.5)
    for k, cols in enumerate(home):
        part = pl.ds(cols[0], cols[1] - cols[0])
        acc[part, :] = jnp.zeros_like(acc[part, :])
        for c in range(0, tx, 4):
            weighted = [
                (vtp[i, part, :].astype(F32) * (pot[i : i + 1, :] * weight)).astype(BF16)
                for i in range(c, c + 4)
            ]
            whole = vp[c : c + 4].reshape(4 * points, orb)
            acc[part, :] += dot(jnp.concatenate(weighted, axis=1), whole)
        tmat[part, :] = acc[part, :].astype(BF16)

        def repack(i, carry, part=part):
            at = pl.ds(pl.multiple_of(i * rows, rows), rows)
            ret_buf[at, part] = dot(hot_in[at, :], tmat[part, :], 1, 1).astype(BF16)
            return carry

        lax.fori_loop(0, tiles * 16 // rows, repack, 0, unroll=True)
        exchange(ret_buf, back_buf, ret_send, ret_recv.at[k], cols)

    high, rest = split(pot[...])
    rest = pot[...] - high.astype(F32)
    mid, low = split(rest)
    natural = dot(high, perm[...]) + (dot(mid, perm[...]) + dot(low, perm[...]))
    for y in range(ty):
        pot_ref[:, y, :] = natural[:, y * tz : (y + 1) * tz]

    for copy in copies:
        copy.wait_send()
    sent = key_out.at[pl.ds(0, tiles - 1)]
    pltpu.make_async_copy(sent, sent, key_send).wait()
    sent = out_buf.at[pl.ds(0, (tiles - 1) * 16), :]
    pltpu.make_async_copy(sent, sent, pay_send).wait()
    for k, cols in enumerate(home):
        own_ref[:, cols[0] : cols[1]] = gathered(hot_out_t, back_buf, ret_recv.at[k], cols).astype(BF16)
    sent = ret_buf.at[pl.ds(0, (tiles - 1) * 16), :]
    pltpu.make_async_copy(sent, sent, ret_send).wait()


def hand_over(pot_ref, own_ref, pot_out, own_out):
    pot_out[...] = pot_ref[...]
    own_out[...] = own_ref[...]


def solution(mesh):
    sizes = tuple(mesh.shape[a] for a in ("gx", "gy", "gz"))

    def local(values, slabs, slab_tile, slab_place):
        tx, ty, tz, orb = values.shape
        count = slabs.shape[0]
        points, tiles = ty * tz, sizes[0] * sizes[1]
        along_x, lanes = filter_tables(tx)
        high = along_x.astype(jnp.bfloat16)
        low = (along_x - high.astype(np.float32)).astype(jnp.bfloat16)
        xmat = np.concatenate([high, high, low], axis=0)
        wide = points + 2 * RADIUS * ty
        vm, any_ = pl.BlockSpec(memory_space=pltpu.VMEM), pl.BlockSpec(memory_space=pl.ANY)
        dma, slots = pltpu.SemaphoreType.DMA, tiles * 16
        pot, own = pl.pallas_call(
            functools.partial(kernel, (sizes, (tx, ty, tz), count, orb)),
            out_shape=(
                jax.ShapeDtypeStruct((tx, ty, tz), F32),
                jax.ShapeDtypeStruct((count * 8, orb), BF16),
            ),
            in_specs=[any_] * 6,
            out_specs=(vm, vm),
            scratch_shapes=[
                pltpu.VMEM((tx, points, orb), BF16),
                pltpu.VMEM((count * 8, orb), BF16),
                pltpu.VMEM((tx, points, orb), BF16),
                pltpu.VMEM((tx, orb, points), BF16),
                pltpu.VMEM((points, points), BF16),
                pltpu.VMEM((slots, orb), BF16),
                pltpu.VMEM((orb, slots), BF16),
                pltpu.VMEM((slots, orb), BF16),
                pltpu.VMEM((orb, slots), BF16),
                pltpu.VMEM((tiles, 1, 128), F32),
                pltpu.VMEM((tiles, 1, 128), F32),
                pltpu.VMEM((slots, orb), BF16),
                pltpu.VMEM((slots, orb), BF16),
                pltpu.VMEM((slots, orb), BF16),
                pltpu.VMEM((slots, orb), BF16),
                pltpu.VMEM((orb, orb), BF16),
                pltpu.VMEM((orb, orb), F32),
                pltpu.VMEM((3, tx + 2 * RADIUS, wide), F32),
                pltpu.VMEM((tz + 2 * RADIUS, ty + 2 * RADIUS, 128), F32),
                pltpu.VMEM((tz, ty + 2 * RADIUS, 128), F32),
                pltpu.VMEM((tx, points), F32),
                pltpu.VMEM((1, count), I32),
                pltpu.VMEM((1, count), I32),
                pltpu.VMEM(xmat.shape, BF16),
                pltpu.VMEM(lanes.shape, F32),
                dma((6,)), dma, dma, dma, dma((2, sizes[0])), dma, dma((2, sizes[0])),
                dma((26,)), dma((26,)),
            ],
            compiler_params=pltpu.CompilerParams(
                collective_id=0, has_side_effects=True, vmem_limit_bytes=56 * 1024 * 1024
            ),
        )(
            values.reshape(tx, points, orb),
            slabs.reshape(count * 8, orb),
            slab_tile.reshape(1, count),
            slab_place.reshape(1, count),
            jnp.asarray(xmat),
            jnp.asarray(lanes),
        )
        pot, own = pl.pallas_call(
            hand_over,
            out_shape=(
                jax.ShapeDtypeStruct((tx, ty, tz), F32),
                jax.ShapeDtypeStruct((count * 8, orb), BF16),
            ),
            in_specs=[vm, vm],
            out_specs=(vm, vm),
        )(pot, own)
        return pot, own.reshape(count, 8, orb)

    return jax.shard_map(
        local,
        mesh=mesh,
        in_specs=(
            P("gx", "gy", "gz", None),
            P(("gx", "gy", "gz"), None, None),
            P(("gx", "gy", "gz")),
            P(("gx", "gy", "gz")),
        ),
        out_specs=(P("gx", "gy", "gz"), P(("gx", "gy", "gz"), None, None)),
        check_vma=False,
    )
```
